512 devices in a mesh: seq: 64 (over y_hi, z, x), head: 8 (over y_lo, core).
Axes of the slice: x: 4, y: 8 (y_hi: 2, y_lo: 4; y = y_hi * 4 + y_lo), z: 8, core: 2. Of those that a mesh axis runs over, the one named last changes fastest.
Arguments:
- fw_query: bfloat16 [24576, 4096], P('seq', 'head'), may hold values from -6 to 6
- fw_key: bfloat16 [24576, 4096], P('seq', 'head'), may hold values from -6 to 6
- fw_value: bfloat16 [24576, 4096], P('seq', 'head'), may hold values from -6 to 6
- learn_rate: float32 [24576, 8], P('seq', 'head'), may hold values from 0.00012757759 to 0.001275776
- fast_weights: bfloat16 [3, 8, 512, 512], P(None, 'head'), may hold values from -0.25 to 0.25
- attn_query: bfloat16 [24576, 4096], P(('seq', 'head')), may hold values from -32 to 32
- attn_key: bfloat16 [24576, 1024], P(('seq', 'head')), may hold values from -32 to 32
- attn_value: bfloat16 [24576, 1024], P(('seq', 'head')), may hold values from -6 to 6
Outputs:
- mixed: bfloat16 [24576, 4096], P(('seq', 'head'))
The draws below stay inside these ranges and needn't reach their ends.
All inputs are finite; a program needn't handle non-finite values.
Results may differ from the reference program's by a relative error of at most 0.01.
Values may be sent and summed in bfloat16 or wider, within the bound.
No kernel may reach another device: no remote copies, remote signals or barrier semaphores. Data moves between devices by JAX's collectives and lax.ppermute only.
A program may use at most 64 MiB of HBM per device.

```python
import math
import jax
import jax.numpy as jnp
from jax import lax

FW_HEADS = 8
FW_DIM = 512
Q_HEADS = 32
KV_HEADS = 8
HEAD_DIM = 128
WINDOW = 256
D = 4096
TOKENS = 24576


def draw_attn_key(key, part):
    base = jax.random.normal(jax.random.fold_in(key, 1), (TOKENS, KV_HEADS * HEAD_DIM), jnp.float32)
    base = jnp.clip(base, -6.0, 6.0)
    return jnp.clip(base, -32.0, 32.0).astype(jnp.bfloat16)


def draw_attn_query(key, part):
    base = jax.random.normal(jax.random.fold_in(key, 2), (TOKENS, Q_HEADS * HEAD_DIM), jnp.float32)
    base = jnp.clip(base, -6.0, 6.0)
    return jnp.clip(base, -32.0, 32.0).astype(jnp.bfloat16)


def shard_levels(stream_key, dims, shards, least, top_value):
    loudness = 1.0
    for dim, blocks in shards:
        draws = jax.random.uniform(jax.random.fold_in(jax.random.fold_in(stream_key, 6), dim), (blocks,), jnp.float32, least / len(shards), top_value / len(shards))
        loudness = loudness * jnp.repeat(jnp.exp(draws), dims[dim] // blocks).reshape((-1,) + (1,) * (len(dims) - 1 - dim))
    return loudness


def noise(rng, shape, scale, most, cuts=(), kind=jnp.bfloat16):
    level = shard_levels(rng, shape, cuts, -0.22, 0.18) if cuts else 1.0
    drawn = jax.random.normal(rng, shape, jnp.float32) * scale * level
    return jnp.minimum(jnp.maximum(drawn, -most), most).astype(kind)


def setup_inputs(seed: int = 0) -> dict:
    key_of = jax.random.split(jax.random.key(seed), 9)
    return {
        "fw_query": noise(key_of[0], (TOKENS, D), 1.0, 6.0, ((0, 64), (1, 8))),
        "fw_key": noise(key_of[1], (TOKENS, D), 1.0, 6.0, ((0, 64), (1, 8))),
        "fw_value": noise(key_of[2], (TOKENS, D), 1.0, 6.0, ((0, 64), (1, 8))),
        "learn_rate": jnp.clip(jnp.exp(math.log(0.001275776) - 2.3025852 * jax.random.uniform(key_of[3], (TOKENS, FW_HEADS), jnp.float32) ** shard_levels(key_of[3], (TOKENS, FW_HEADS), ((0, 64), (1, 8)), -0.2, 0.2)), 0.00012757759, 0.001275776),
        "fast_weights": noise(key_of[4], (3, FW_HEADS, FW_DIM, FW_DIM), FW_DIM ** -0.5, 0.25, ((1, 8),)),
        "attn_query": draw_attn_query(jax.random.fold_in(key_of[8], 71), 0),
        "attn_key": draw_attn_key(jax.random.fold_in(key_of[8], 71), 0),
        "attn_value": noise(key_of[7], (TOKENS, KV_HEADS * HEAD_DIM), 1.0, 6.0, ((0, 512),)),
    }


def head_update(q, k, v, rates, weights):
    w_gate = weights[0]
    w_up = weights[1]
    w_down = weights[2]
    pre_gate = jnp.dot(k, w_gate, preferred_element_type=jnp.float32)
    pre_up = jnp.dot(k, w_up, preferred_element_type=jnp.float32)
    sigm = jax.nn.sigmoid(pre_gate)
    hidden = (pre_gate * sigm * pre_up).astype(jnp.bfloat16)
    scaled = (rates[:, None] * v.astype(jnp.float32)).astype(jnp.bfloat16)
    back = jnp.dot(scaled, w_down.T, preferred_element_type=jnp.float32)
    d_gate = (back * pre_up * sigm * (1.0 + pre_gate * (1.0 - sigm))).astype(jnp.bfloat16)
    d_up = (back * pre_gate * sigm).astype(jnp.bfloat16)
    grads = jnp.stack([jnp.dot(k.T, d_gate, preferred_element_type=jnp.float32), jnp.dot(k.T, d_up, preferred_element_type=jnp.float32), jnp.dot(hidden.T, scaled, preferred_element_type=jnp.float32)])
    start = weights.astype(jnp.float32)
    stepped = start + grads
    ratio = jnp.sqrt(lax.optimization_barrier(jnp.mean(start * start, axis=-2, keepdims=True))) * lax.rsqrt(lax.optimization_barrier(jnp.mean(stepped * stepped, axis=-2, keepdims=True)) + 1e-06)
    fresh = (stepped * ratio).astype(jnp.bfloat16)
    q_gate = jnp.dot(q, fresh[0], preferred_element_type=jnp.float32)
    q_up = jnp.dot(q, fresh[1], preferred_element_type=jnp.float32)
    answer_hidden = (q_gate * jax.nn.sigmoid(q_gate) * q_up).astype(jnp.bfloat16)
    return jnp.dot(answer_hidden, fresh[2], preferred_element_type=jnp.float32).astype(jnp.bfloat16)

def reference(fw_query, fw_key, fw_value, learn_rate, fast_weights, attn_query, attn_key, attn_value):

    def heads_first(arr):
        return arr.reshape(TOKENS, FW_HEADS, FW_DIM).transpose(1, 0, 2)

    def per_head(items):
        return head_update(items[0], items[1], items[2], items[3], items[4])
    fw_heads = lax.map(per_head, (heads_first(fw_query), heads_first(fw_key), heads_first(fw_value), learn_rate.T, fast_weights.transpose(1, 0, 2, 3)))
    fw_out = fw_heads.transpose(1, 0, 2).reshape(TOKENS, D)
    group = Q_HEADS // KV_HEADS
    block_rows = math.gcd(512, TOKENS)
    scaling = 1.0 / math.sqrt(HEAD_DIM)
    query_heads = attn_query.reshape(TOKENS, KV_HEADS, group, HEAD_DIM)
    front = jnp.zeros((WINDOW, KV_HEADS * HEAD_DIM), jnp.bfloat16)
    key_pad = jnp.concatenate([front, attn_key], axis=0).reshape(TOKENS + WINDOW, KV_HEADS, HEAD_DIM)
    value_pad = jnp.concatenate([front, attn_value], axis=0).reshape(TOKENS + WINDOW, KV_HEADS, HEAD_DIM)

    def block(index):
        start = (index * block_rows).astype(jnp.int32)
        q_block = lax.dynamic_slice_in_dim(query_heads, start, block_rows, 0)
        k_block = lax.dynamic_slice_in_dim(key_pad, start, block_rows + WINDOW, 0)
        v_block = lax.dynamic_slice_in_dim(value_pad, start, block_rows + WINDOW, 0)
        scores = jnp.einsum('fcgd,lcd->cgfl', q_block.astype(jnp.float32), k_block.astype(jnp.float32)) * scaling
        t_pos = start + jnp.arange(block_rows, dtype=jnp.int32)
        s_pos = start - WINDOW + jnp.arange(block_rows + WINDOW, dtype=jnp.int32)
        gap = t_pos[:, None] - s_pos[None, :]
        keep = (gap >= 0) & (gap < WINDOW) & (s_pos[None, :] >= 0)
        scores = jnp.where(keep, scores, -1e+30)
        top = lax.optimization_barrier(jnp.max(scores, axis=-1, keepdims=True))
        expo = jnp.exp(scores - top)
        probs = (expo / lax.optimization_barrier(jnp.sum(expo, axis=-1, keepdims=True))).astype(jnp.bfloat16)
        out = jnp.einsum('cgfl,lcd->fcgd', probs.astype(jnp.float32), v_block.astype(jnp.float32))
        return out.reshape(block_rows, Q_HEADS * HEAD_DIM)
    attn_out = lax.map(block, jnp.arange(TOKENS // block_rows, dtype=jnp.int32)).reshape(TOKENS, D)
    return (attn_out + fw_out.astype(jnp.float32)).astype(jnp.bfloat16)
```

```python
import math

import jax
import jax.numpy as jnp
from jax import lax
from jax.sharding import Mesh, PartitionSpec as P

Q_HEADS = 32
KV_HEADS = 8
HEAD_DIM = 128
WINDOW = 256

FINE = (("yh", 2), ("zh", 4), ("zl", 2), ("x", 4), ("yl", 4), ("core", 2))
SEQ = ("yh", "zh", "zl", "x")
HEAD = ("yl", "core")
INNER = ("x",)
OUTER = ("yh", "zh", "zl")


def shifted(value, by):
    axes = SEQ + HEAD
    devices = lax.axis_size(axes)
    return lax.ppermute(value, axes, [(i, i + by) for i in range(devices - by)])


def spread(value, axes):
    devices = lax.axis_size(axes)
    many = jnp.broadcast_to(value[None], (devices,) + value.shape)
    return lax.all_to_all(many, axes, 0, 0, tiled=True)


def local_grads(keys, values, rates, weights):
    pre_gate = jnp.dot(keys, weights[0], preferred_element_type=jnp.float32)
    pre_up = jnp.dot(keys, weights[1], preferred_element_type=jnp.float32)
    sigm = jax.nn.sigmoid(pre_gate)
    hidden = (pre_gate * sigm * pre_up).astype(jnp.bfloat16)
    scaled = (rates * values.astype(jnp.float32)).astype(jnp.bfloat16)
    back = jnp.einsum("te,de->td", scaled, weights[2], preferred_element_type=jnp.float32)
    d_gate = (back * pre_up * sigm * (1.0 + pre_gate * (1.0 - sigm))).astype(jnp.bfloat16)
    d_up = (back * pre_gate * sigm).astype(jnp.bfloat16)

    def product(left, right):
        return jnp.einsum("te,td->ed", left, right, preferred_element_type=jnp.float32)

    return product(d_gate, keys), product(d_up, keys), product(scaled, hidden)


def on_device(
    fw_query, fw_key, fw_value, learn_rate, fast_weights, attn_query, attn_key, attn_value
):
    rows = attn_query.shape[0]
    kv = jnp.concatenate([attn_key, attn_value], axis=1)
    one = shifted(kv, 1)
    two = shifted(jnp.concatenate([one, kv]), 2)
    three = shifted(jnp.concatenate([two[rows:], one, kv]), 4)
    near = jnp.concatenate([three, two, one, kv])

    weights = fast_weights[:, 0]
    width = weights.shape[1]
    inner, outer = lax.axis_size(INNER), lax.axis_size(OUTER)
    part = width // (inner * outer)
    grads = local_grads(fw_key, fw_value, learn_rate, weights)
    pieces = jnp.stack(
        [g.astype(jnp.bfloat16).reshape(inner, outer, part, width) for g in grads], axis=2
    )
    pieces = lax.all_to_all(pieces, INNER, 0, 0, tiled=True)
    pieces = jnp.sum(pieces.astype(jnp.float32), axis=0).astype(jnp.bfloat16)
    pieces = lax.all_to_all(pieces, OUTER, 0, 0, tiled=True)
    summed = jnp.sum(pieces.astype(jnp.float32), axis=0)

    mine = (lax.axis_index(INNER) * outer + lax.axis_index(OUTER)) * part
    start = lax.dynamic_slice_in_dim(weights, mine, part, 2).transpose(0, 2, 1)
    start = start.astype(jnp.float32)
    stepped = start + summed
    ratio = jnp.sqrt(jnp.mean(start * start, axis=-1, keepdims=True)) * lax.rsqrt(
        jnp.mean(stepped * stepped, axis=-1, keepdims=True) + 1e-06
    )
    fresh = (stepped * ratio).astype(jnp.bfloat16)
    fresh = spread(spread(fresh, OUTER), INNER)
    fresh = fresh.reshape(inner * outer, 3, part, width)
    new_gate, new_up, new_down = (fresh[:, m].reshape(width, width) for m in range(3))

    def product(left, right):
        return jnp.einsum("td,ed->te", left, right, preferred_element_type=jnp.float32)

    q_gate = product(fw_query, new_gate)
    q_up = product(fw_query, new_up)
    answer_hidden = (q_gate * jax.nn.sigmoid(q_gate) * q_up).astype(jnp.bfloat16)
    fw_out = product(answer_hidden, new_down).astype(jnp.bfloat16)
    fw_fine = lax.all_to_all(fw_out.reshape(-1, rows, width), HEAD, 0, 0, tiled=True)
    fw_fine = fw_fine.transpose(1, 0, 2).reshape(rows, -1)

    span = near.shape[0]
    near_k, near_v = (near[:, i * 1024 : (i + 1) * 1024] for i in range(2))
    near_k = near_k.reshape(span, KV_HEADS, HEAD_DIM)
    near_v = near_v.reshape(span, KV_HEADS, HEAD_DIM)
    group = Q_HEADS // KV_HEADS
    t_pos = lax.axis_index(SEQ + HEAD) * rows + jnp.arange(rows, dtype=jnp.int32)
    s_pos = lax.axis_index(SEQ + HEAD) * rows + rows - span + jnp.arange(span, dtype=jnp.int32)
    gap = t_pos[:, None] - s_pos[None, :]
    keep = (gap >= 0) & (gap < WINDOW) & (s_pos[None, :] >= 0)
    query_heads = attn_query.reshape(rows, KV_HEADS, group, HEAD_DIM)
    scaling = 1.0 / math.sqrt(HEAD_DIM)
    scores = (
        jnp.einsum("fcgd,lcd->cgfl", query_heads, near_k, preferred_element_type=jnp.float32)
        * scaling
    )
    scores = jnp.where(keep, scores, -1e30)
    top = jnp.max(scores, axis=-1, keepdims=True)
    expo = jnp.exp(scores - top)
    probs = (expo / jnp.sum(expo, axis=-1, keepdims=True)).astype(jnp.bfloat16)
    attn_out = jnp.einsum("cgfl,lcd->fcgd", probs, near_v, preferred_element_type=jnp.float32)
    attn_out = attn_out.reshape(rows, Q_HEADS * HEAD_DIM)
    return (attn_out + fw_fine.astype(jnp.float32)).astype(jnp.bfloat16)


def solution(mesh):
    fine = Mesh(
        mesh.devices.reshape([size for _, size in FINE]), tuple(name for name, _ in FINE)
    )
    placed = (
        P(SEQ, HEAD),
        P(SEQ, HEAD),
        P(SEQ, HEAD),
        P(SEQ, HEAD),
        P(None, HEAD, None, None),
        P(SEQ + HEAD, None),
        P(SEQ + HEAD, None),
        P(SEQ + HEAD, None),
    )
    return jax.shard_map(
        on_device, mesh=fine, in_specs=placed, out_specs=P(SEQ + HEAD, None), check_vma=False
    )
```

```python
import functools
import math

import jax
import jax.numpy as jnp
from jax import lax
from jax.experimental import pallas as pl
from jax.experimental.pallas import tpu as pltpu
from jax.sharding import Mesh, PartitionSpec as P

Q_HEADS = 32
KV_HEADS = 8
HEAD_DIM = 128
WINDOW = 256
MIB = 1 << 20

FINE = (("yh", 2), ("zh", 4), ("zl", 2), ("xh", 2), ("xl", 2), ("yl", 4), ("core", 2))
SEQ = ("yh", "zh", "zl", "xh", "xl")
HEAD = ("yl", "core")
NEAR = ("zl", "xl")
FAR = ("zh", "xh")

F32 = jnp.float32
BF16 = jnp.bfloat16
ROWS_ROWS = (((0,), (0,)), ((), ()))
COLS_COLS = (((1,), (1,)), ((), ()))


def next_chip(value):
    axes = SEQ + HEAD
    devices = lax.axis_size(axes)
    return lax.ppermute(value, axes, [(i, i + 2) for i in range(devices - 2)])


def swapped(value, axis):
    return lax.ppermute(value, axis, [(0, 1), (1, 0)])


def after(value, first):
    return lax.optimization_barrier((value, first))


def call(body, out, args, mib, flops=0):
    moved = sum(a.size * a.dtype.itemsize for a in args) + out.size * out.dtype.itemsize
    return pl.pallas_call(
        body,
        out_shape=out,
        compiler_params=pltpu.CompilerParams(vmem_limit_bytes=mib * MIB),
        cost_estimate=pl.CostEstimate(flops=flops, bytes_accessed=moved, transcendentals=0),
    )(*args)


def dot(left, right, dims=(((1,), (0,)), ((), ()))):
    return lax.dot_general(left, right, dims, preferred_element_type=F32)


def grads_body(k_ref, v_ref, rate_ref, w_ref, out_ref):
    close, far, _, part, width = out_ref.shape
    block = width // 2
    keys = k_ref[...]
    rates = rate_ref[...].reshape(keys.shape[0], 1)
    scaled = (rates * v_ref[...].astype(F32)).astype(BF16)
    for start in range(0, width, block):
        cols = slice(start, start + block)
        gate = dot(keys, w_ref[0, :, cols])
        up = dot(keys, w_ref[1, :, cols])
        back = dot(scaled, w_ref[2, cols, :], COLS_COLS)
        sigm = jax.nn.sigmoid(gate)
        act = gate * sigm
        hidden = (act * up).astype(BF16)
        d_gate = (back * up * sigm * (1.0 + gate * (1.0 - sigm))).astype(BF16)
        d_up = (back * act).astype(BF16)
        half = slice(start * close // width, (start + block) * close // width)
        shape = (close * block // width, far, part, width)
        out_ref[half, :, 0] = dot(d_gate, keys, ROWS_ROWS).astype(BF16).reshape(shape)
        out_ref[half, :, 1] = dot(d_up, keys, ROWS_ROWS).astype(BF16).reshape(shape)
        down = dot(scaled, hidden, ROWS_ROWS).astype(BF16)
        out_ref[:, :, 2, :, cols] = down.reshape(close, far, part, block)


def sum_body(in_ref, out_ref):
    total = in_ref[0].astype(F32)
    for i in range(1, in_ref.shape[0]):
        total = total + in_ref[i].astype(F32)
    out_ref[...] = total.astype(out_ref.dtype)


def renorm_body(half_ref, other_ref, start_ref, out_ref):
    start = start_ref[...].astype(F32)
    stepped = start + (half_ref[...] + other_ref[...])
    ratio = jnp.sqrt(jnp.mean(start * start, axis=-1, keepdims=True)) * lax.rsqrt(
        jnp.mean(stepped * stepped, axis=-1, keepdims=True) + 1e-06
    )
    fresh = (stepped * ratio).astype(BF16)
    for i in range(out_ref.shape[0]):
        out_ref[i] = fresh


def copies_body(in_ref, out_ref):
    for i in range(out_ref.shape[0]):
        out_ref[i] = in_ref[...]


def answer_body(q_ref, w_ref, out_ref):
    width = q_ref.shape[1]
    query = q_ref[...]
    gate_w, up_w, down_w = (w_ref[:, :, m].reshape(width, width) for m in range(3))
    gate = dot(query, gate_w, COLS_COLS)
    up = dot(query, up_w, COLS_COLS)
    hidden = (gate * jax.nn.sigmoid(gate) * up).astype(BF16)
    out_ref[...] = dot(hidden, down_w, COLS_COLS).astype(BF16).reshape(out_ref.shape)


def attend_body(place_ref, q_ref, *refs):
    *kv_refs, swap_ref, out_ref = refs
    rows = q_ref.shape[0]
    links = len(kv_refs)
    span = 2 * links * rows
    group = Q_HEADS // KV_HEADS
    kv_width = KV_HEADS * HEAD_DIM
    device, other = place_ref[0], place_ref[1]
    key = lax.broadcasted_iota(jnp.int32, (1, span), 1)
    s_pos = key + device * rows
    for i in range(1, 2 * links):
        origin = device - 2 * i if i < links else other - 2 * (i - links)
        s_pos = jnp.where(key >= i * rows, key + (origin - i) * rows, s_pos)
    t_pos = device * rows + lax.broadcasted_iota(jnp.int32, (rows, 1), 0)
    gap = t_pos - s_pos
    keep = (gap >= 0) & (gap < WINDOW) & (s_pos >= 0)
    keep = jnp.concatenate([keep] * group, axis=0)
    scaling = 1.0 / math.sqrt(HEAD_DIM)
    for c in range(KV_HEADS):
        own = slice(c * HEAD_DIM, (c + 1) * HEAD_DIM)
        vals = slice(kv_width + c * HEAD_DIM, kv_width + (c + 1) * HEAD_DIM)
        keys = jnp.concatenate([r[:, own] for r in kv_refs] + [swap_ref[:, own]], axis=0)
        values = jnp.concatenate([r[:, vals] for r in kv_refs] + [swap_ref[:, vals]], axis=0)
        heads = [slice((c * group + j) * HEAD_DIM, (c * group + j + 1) * HEAD_DIM) for j in range(group)]
        query = jnp.concatenate([q_ref[:, h] for h in heads], axis=0)
        scores = jnp.where(keep, dot(query, keys, COLS_COLS) * scaling, -1e30)
        expo = jnp.exp(scores - jnp.max(scores, axis=-1, keepdims=True))
        probs = (expo / jnp.sum(expo, axis=-1, keepdims=True)).astype(BF16)
        result = dot(probs, values)
        for j, h in enumerate(heads):
            out_ref[:, h] = result[j * rows : (j + 1) * rows]


def mix_body(attn_ref, fw_ref, out_ref):
    width = fw_ref.shape[2]
    for h in range(fw_ref.shape[0]):
        cols = slice(h * width, (h + 1) * width)
        out_ref[:, cols] = (attn_ref[:, cols] + fw_ref[h].astype(F32)).astype(BF16)


def on_device(
    fw_query, fw_key, fw_value, learn_rate, fast_weights, attn_query, attn_key, attn_value
):
    rows = attn_query.shape[0]
    tok_rows, width = fw_key.shape
    weights = fast_weights[:, 0]
    close, far = lax.axis_size(NEAR), lax.axis_size(FAR)
    part = width // (close * far)
    shape = jax.ShapeDtypeStruct
    product = 2 * tok_rows * width * width

    kv = [jnp.concatenate([attn_key, attn_value], axis=1)]
    pieces = call(
        grads_body,
        shape((close, far, 3, part, width), BF16),
        (fw_key, fw_value, learn_rate.reshape(1, tok_rows), weights),
        32,
        6 * product,
    )
    pieces = lax.all_to_all(pieces, NEAR, 0, 0, tiled=True)
    kv.append(next_chip(kv[-1]))
    pieces, kv[-1] = after(pieces, kv[-1])
    pieces = call(sum_body, shape((far, 3, part, width), BF16), (pieces,), 16)
    pieces = lax.all_to_all(pieces, FAR, 0, 0, tiled=True)
    half = call(sum_body, shape((3, part, width), F32), (pieces,), 16)
    kv.append(next_chip(kv[-1]))
    half, kv[-1] = after(half, kv[-1])

    mine = (lax.axis_index(NEAR) * far + lax.axis_index(FAR)) * part
    start = lax.dynamic_slice_in_dim(weights, mine, part, 2).transpose(0, 2, 1)
    other = swapped(half, "yh")
    fresh = call(renorm_body, shape((far, 3, part, width), BF16), (half, other, start), 16)
    fresh = lax.all_to_all(fresh, FAR, 0, 0, tiled=True)
    kv.append(next_chip(kv[-1]))
    fresh, kv[-1] = after(fresh, kv[-1])
    fresh = call(copies_body, shape((close, far, 3, part, width), BF16), (fresh,), 16)
    fresh = lax.all_to_all(fresh, NEAR, 0, 0, tiled=True)
    swap = swapped(jnp.concatenate(kv), "core")

    fw_out = call(
        answer_body,
        shape((tok_rows // rows, rows, width), BF16),
        (fw_query, fresh),
        24,
        3 * product,
    )
    fw_fine = lax.all_to_all(fw_out, HEAD, 0, 0, tiled=True)
    device = lax.axis_index(SEQ + HEAD)
    place = jnp.stack([device, device + 1 - 2 * lax.axis_index("core")])
    attn = pl.pallas_call(
        attend_body,
        out_shape=shape(attn_query.shape, F32),
        in_specs=[pl.BlockSpec(memory_space=pltpu.SMEM)]
        + [pl.BlockSpec(memory_space=pltpu.VMEM)] * (len(kv) + 2),
        compiler_params=pltpu.CompilerParams(vmem_limit_bytes=24 * MIB),
        cost_estimate=pl.CostEstimate(flops=10**9, bytes_accessed=3 * MIB, transcendentals=0),
    )(place, attn_query, *kv, swap)
    return call(mix_body, shape(attn_query.shape, BF16), (attn, fw_fine), 16)


def solution(mesh):
    fine = Mesh(
        mesh.devices.reshape([size for _, size in FINE]), tuple(name for name, _ in FINE)
    )
    placed = (
        P(SEQ, HEAD),
        P(SEQ, HEAD),
        P(SEQ, HEAD),
        P(SEQ, HEAD),
        P(None, HEAD, None, None),
        P(SEQ + HEAD, None),
        P(SEQ + HEAD, None),
        P(SEQ + HEAD, None),
    )
    return jax.shard_map(
        on_device, mesh=fine, in_specs=placed, out_specs=P(SEQ + HEAD, None), check_vma=False
    )
```

```python
import functools
import math

import jax
import jax.numpy as jnp
from jax import lax
from jax.experimental import pallas as pl
from jax.experimental.pallas import tpu as pltpu
from jax.sharding import Mesh, PartitionSpec as P

Q_HEADS = 32
KV_HEADS = 8
HEAD_DIM = 128
WINDOW = 256
MIB = 1 << 20

FINE = (("yh", 2), ("zh", 4), ("zl", 2), ("x", 4), ("yl", 4), ("core", 2))
SEQ = ("yh", "zh", "zl", "x")
HEAD = ("yl", "core")
NEAR = ("zl", "x")
FAR = ("zh",)

F32 = jnp.float32
BF16 = jnp.bfloat16
ROWS_ROWS = (((0,), (0,)), ((), ()))
COLS_COLS = (((1,), (1,)), ((), ()))


def next_chip(value):
    axes = SEQ + HEAD
    devices = lax.axis_size(axes)
    return lax.ppermute(value, axes, [(i, i + 2) for i in range(devices - 2)])


def swapped(value, axis):
    return lax.ppermute(value, axis, [(0, 1), (1, 0)])


def after(value, first):
    return lax.optimization_barrier((value, first))


def call(body, out, args, mib, flops=0):
    moved = sum(a.size * a.dtype.itemsize for a in args) + out.size * out.dtype.itemsize
    return pl.pallas_call(
        body,
        out_shape=out,
        compiler_params=pltpu.CompilerParams(vmem_limit_bytes=mib * MIB),
        cost_estimate=pl.CostEstimate(flops=flops, bytes_accessed=moved, transcendentals=0),
    )(*args)


def dot(left, right, dims=(((1,), (0,)), ((), ()))):
    return lax.dot_general(left, right, dims, preferred_element_type=F32)


def grads_body(k_hbm, v_hbm, rate_ref, w_hbm, out_ref, k_ref, v_ref, w_ref, sems):
    close, far, _, part, width = out_ref.shape
    block = width // 2
    copies = [
        pltpu.make_async_copy(source, target, sems.at[i])
        for i, (source, target) in enumerate(
            (
                (k_hbm, k_ref),
                (w_hbm.at[0], w_ref.at[0]),
                (w_hbm.at[1], w_ref.at[1]),
                (v_hbm, v_ref),
                (w_hbm.at[2], w_ref.at[2]),
            )
        )
    ]
    for copy in copies:
        copy.start()
    copies[0].wait()
    copies[1].wait()
    keys = k_ref[...]
    for start in range(0, width, block):
        cols = slice(start, start + block)
        gate = dot(keys, w_ref[0, :, cols])
        if start == 0:
            copies[2].wait()
        up = dot(keys, w_ref[1, :, cols])
        if start == 0:
            copies[3].wait()
            rates = rate_ref[...].reshape(keys.shape[0], 1)
            scaled = (rates * v_ref[...].astype(F32)).astype(BF16)
            copies[4].wait()
        back = dot(scaled, w_ref[2, cols, :], COLS_COLS)
        sigm = jax.nn.sigmoid(gate)
        act = gate * sigm
        hidden = (act * up).astype(BF16)
        d_gate = (back * up * sigm * (1.0 + gate * (1.0 - sigm))).astype(BF16)
        d_up = (back * act).astype(BF16)
        half = slice(start * close // width, (start + block) * close // width)
        shape = (close * block // width, far, part, width)
        out_ref[half, :, 0] = dot(d_gate, keys, ROWS_ROWS).astype(BF16).reshape(shape)
        out_ref[half, :, 1] = dot(d_up, keys, ROWS_ROWS).astype(BF16).reshape(shape)
        down = dot(scaled, hidden, ROWS_ROWS).astype(BF16)
        out_ref[:, :, 2, :, cols] = down.reshape(close, far, part, block)


def sum_body(in_ref, out_ref):
    total = in_ref[0].astype(F32)
    for i in range(1, in_ref.shape[0]):
        total = total + in_ref[i].astype(F32)
    out_ref[...] = total.astype(out_ref.dtype)


def renorm_body(half_ref, other_ref, start_ref, out_ref):
    start = start_ref[...].astype(F32)
    stepped = start + (half_ref[...] + other_ref[...])
    ratio = jnp.sqrt(jnp.mean(start * start, axis=-1, keepdims=True)) * lax.rsqrt(
        jnp.mean(stepped * stepped, axis=-1, keepdims=True) + 1e-06
    )
    fresh = (stepped * ratio).astype(BF16)
    for i in range(out_ref.shape[0]):
        out_ref[i] = fresh


def copies_body(in_ref, out_ref):
    for i in range(out_ref.shape[0]):
        out_ref[i] = in_ref[...]


def answer_body(q_ref, w_ref, out_ref):
    width = q_ref.shape[1]
    query = q_ref[...]
    gate_w, up_w, down_w = (w_ref[:, :, m].reshape(width, width) for m in range(3))
    gate = dot(query, gate_w, COLS_COLS)
    up = dot(query, up_w, COLS_COLS)
    hidden = (gate * jax.nn.sigmoid(gate) * up).astype(BF16)
    out_ref[...] = dot(hidden, down_w, COLS_COLS).astype(BF16).reshape(out_ref.shape)


def attend_body(place_ref, q_ref, *refs):
    *kv_refs, swap_ref, out_ref = refs
    rows = q_ref.shape[0]
    links = len(kv_refs)
    span = 2 * links * rows
    group = Q_HEADS // KV_HEADS
    kv_width = KV_HEADS * HEAD_DIM
    device, other = place_ref[0], place_ref[1]
    key = lax.broadcasted_iota(jnp.int32, (1, span), 1)
    s_pos = key + device * rows
    for i in range(1, 2 * links):
        origin = device - 2 * i if i < links else other - 2 * (i - links)
        s_pos = jnp.where(key >= i * rows, key + (origin - i) * rows, s_pos)
    t_pos = device * rows + lax.broadcasted_iota(jnp.int32, (rows, 1), 0)
    gap = t_pos - s_pos
    keep = (gap >= 0) & (gap < WINDOW) & (s_pos >= 0)
    keep = jnp.concatenate([keep] * group, axis=0)
    scaling = 1.0 / math.sqrt(HEAD_DIM)
    for c in range(KV_HEADS):
        own = slice(c * HEAD_DIM, (c + 1) * HEAD_DIM)
        vals = slice(kv_width + c * HEAD_DIM, kv_width + (c + 1) * HEAD_DIM)
        keys = jnp.concatenate([r[:, own] for r in kv_refs] + [swap_ref[:, own]], axis=0)
        values = jnp.concatenate([r[:, vals] for r in kv_refs] + [swap_ref[:, vals]], axis=0)
        heads = [slice((c * group + j) * HEAD_DIM, (c * group + j + 1) * HEAD_DIM) for j in range(group)]
        query = jnp.concatenate([q_ref[:, h] for h in heads], axis=0)
        scores = jnp.where(keep, dot(query, keys, COLS_COLS) * scaling, -1e30)
        expo = jnp.exp(scores - jnp.max(scores, axis=-1, keepdims=True))
        probs = (expo / jnp.sum(expo, axis=-1, keepdims=True)).astype(BF16)
        result = dot(probs, values)
        for j, h in enumerate(heads):
            out_ref[:, h] = result[j * rows : (j + 1) * rows]


def mix_body(attn_ref, fw_ref, out_ref):
    width = fw_ref.shape[2]
    for h in range(fw_ref.shape[0]):
        cols = slice(h * width, (h + 1) * width)
        out_ref[:, cols] = (attn_ref[:, cols] + fw_ref[h].astype(F32)).astype(BF16)


def on_device(
    fw_query, fw_key, fw_value, learn_rate, fast_weights, attn_query, attn_key, attn_value
):
    rows = attn_query.shape[0]
    tok_rows, width = fw_key.shape
    weights = fast_weights[:, 0]
    close, far = lax.axis_size(NEAR), lax.axis_size(FAR)
    part = width // (close * far)
    shape = jax.ShapeDtypeStruct
    product = 2 * tok_rows * width * width

    kv = [jnp.concatenate([attn_key, attn_value], axis=1)]
    hbm = pl.BlockSpec(memory_space=pltpu.HBM)
    vmem = pl.BlockSpec(memory_space=pltpu.VMEM)
    pieces = pl.pallas_call(
        grads_body,
        out_shape=shape((close, far, 3, part, width), BF16),
        in_specs=[hbm, hbm, vmem, hbm],
        scratch_shapes=[
            pltpu.VMEM((tok_rows, width), BF16),
            pltpu.VMEM((tok_rows, width), BF16),
            pltpu.VMEM((3, width, width), BF16),
            pltpu.SemaphoreType.DMA((5,)),
        ],
        compiler_params=pltpu.CompilerParams(vmem_limit_bytes=60 * MIB),
        cost_estimate=pl.CostEstimate(flops=6 * product, bytes_accessed=4 * MIB, transcendentals=0),
    )(fw_key, fw_value, learn_rate.reshape(1, tok_rows), weights)
    pieces = lax.all_to_all(pieces, NEAR, 0, 0, tiled=True)
    kv.append(next_chip(kv[-1]))
    pieces, kv[-1] = after(pieces, kv[-1])
    pieces = call(sum_body, shape((far, 3, part, width), BF16), (pieces,), 16)
    pieces = lax.all_to_all(pieces, FAR, 0, 0, tiled=True)
    half = call(sum_body, shape((3, part, width), F32), (pieces,), 16)

    mine = (lax.axis_index(NEAR) * far + lax.axis_index(FAR)) * part
    start = lax.dynamic_slice_in_dim(weights, mine, part, 2).transpose(0, 2, 1)
    other = swapped(half, "yh")
    kv.append(next_chip(kv[-1]))
    other, kv[-1] = after(other, kv[-1])
    fresh = call(renorm_body, shape((far, 3, part, width), BF16), (half, other, start), 16)
    fresh = lax.all_to_all(fresh, FAR, 0, 0, tiled=True)
    kv.append(next_chip(kv[-1]))
    fresh, kv[-1] = after(fresh, kv[-1])
    fresh = call(copies_body, shape((close, far, 3, part, width), BF16), (fresh,), 16)
    fresh = lax.all_to_all(fresh, NEAR, 0, 0, tiled=True)
    swap = swapped(jnp.concatenate(kv), "core")

    fw_out = call(
        answer_body,
        shape((tok_rows // rows, rows, width), BF16),
        (fw_query, fresh),
        24,
        3 * product,
    )
    fw_fine = lax.all_to_all(fw_out, HEAD, 0, 0, tiled=True)
    device = lax.axis_index(SEQ + HEAD)
    place = jnp.stack([device, device + 1 - 2 * lax.axis_index("core")])
    attn = pl.pallas_call(
        attend_body,
        out_shape=shape(attn_query.shape, F32),
        in_specs=[pl.BlockSpec(memory_space=pltpu.SMEM)]
        + [pl.BlockSpec(memory_space=pltpu.VMEM)] * (len(kv) + 2),
        compiler_params=pltpu.CompilerParams(vmem_limit_bytes=24 * MIB),
        cost_estimate=pl.CostEstimate(flops=10**9, bytes_accessed=3 * MIB, transcendentals=0),
    )(place, attn_query, *kv, swap)
    return call(mix_body, shape(attn_query.shape, BF16), (attn, fw_fine), 16)


def solution(mesh):
    fine = Mesh(
        mesh.devices.reshape([size for _, size in FINE]), tuple(name for name, _ in FINE)
    )
    placed = (
        P(SEQ, HEAD),
        P(SEQ, HEAD),
        P(SEQ, HEAD),
        P(SEQ, HEAD),
        P(None, HEAD, None, None),
        P(SEQ + HEAD, None),
        P(SEQ + HEAD, None),
        P(SEQ + HEAD, None),
    )
    return jax.shard_map(
        on_device, mesh=fine, in_specs=placed, out_specs=P(SEQ + HEAD, None), check_vma=False
    )
```

```python
import functools
import math

import jax
import jax.numpy as jnp
from jax import lax
from jax.experimental import pallas as pl
from jax.experimental.pallas import tpu as pltpu
from jax.sharding import Mesh, PartitionSpec as P

Q_HEADS = 32
KV_HEADS = 8
HEAD_DIM = 128
WINDOW = 256
MIB = 1 << 20

FINE = (("yh", 2), ("zh", 4), ("zl", 2), ("x", 4), ("yl", 4), ("core", 2))
SEQ = ("yh", "zh", "zl", "x")
HEAD = ("yl", "core")
NEAR = ("zl", "x")
FAR = ("zh",)

F32 = jnp.float32
BF16 = jnp.bfloat16
ROWS_ROWS = (((0,), (0,)), ((), ()))
COLS_COLS = (((1,), (1,)), ((), ()))


def next_chip(value):
    axes = SEQ + HEAD
    devices = lax.axis_size(axes)
    return lax.ppermute(value, axes, [(i, i + 2) for i in range(devices - 2)])


def swapped(value, axis):
    return lax.ppermute(value, axis, [(0, 1), (1, 0)])


def after(value, first):
    return lax.optimization_barrier((value, first))


def call(body, out, args, mib, flops=0):
    moved = sum(a.size * a.dtype.itemsize for a in args) + out.size * out.dtype.itemsize
    return pl.pallas_call(
        body,
        out_shape=out,
        compiler_params=pltpu.CompilerParams(vmem_limit_bytes=mib * MIB),
        cost_estimate=pl.CostEstimate(flops=flops, bytes_accessed=moved, transcendentals=0),
    )(*args)


def dot(left, right, dims=(((1,), (0,)), ((), ()))):
    return lax.dot_general(left, right, dims, preferred_element_type=F32)


def grads_body(
    k_hbm, v_hbm, rate_ref, w_hbm, out_hbm, k_ref, v_ref, w_ref, out_ref, in_sems, out_sems
):
    close, far, _, part, width = out_hbm.shape
    sources = (k_hbm, w_hbm.at[0], w_hbm.at[1], v_hbm, w_hbm.at[2])
    targets = (k_ref, w_ref.at[0], w_ref.at[1], v_ref, w_ref.at[2])
    copies = [
        pltpu.make_async_copy(source, target, in_sems.at[i])
        for i, (source, target) in enumerate(zip(sources, targets))
    ]
    for copy in copies:
        copy.start()

    def send(m, left, right):
        grad = dot(left, right, ROWS_ROWS).astype(BF16)
        out_ref[m] = grad.reshape(close, far, part, width)
        copy = pltpu.make_async_copy(out_ref.at[m], out_hbm.at[:, :, m], out_sems.at[m])
        copy.start()
        return copy

    copies[0].wait()
    copies[1].wait()
    keys = k_ref[...]
    gate = dot(keys, w_ref[0])
    copies[2].wait()
    up = dot(keys, w_ref[1])
    copies[3].wait()
    rates = rate_ref[...].reshape(keys.shape[0], 1)
    scaled = (rates * v_ref[...].astype(F32)).astype(BF16)
    sigm = jax.nn.sigmoid(gate)
    act = gate * sigm
    sent = [send(2, scaled, (act * up).astype(BF16))]
    copies[4].wait()
    back = dot(scaled, w_ref[2], COLS_COLS)
    sent.append(send(1, (back * act).astype(BF16), keys))
    d_gate = (back * up * sigm * (1.0 + gate * (1.0 - sigm))).astype(BF16)
    sent.append(send(0, d_gate, keys))
    for copy in sent:
        copy.wait()


def sum_body(in_ref, out_ref):
    total = in_ref[0].astype(F32)
    for i in range(1, in_ref.shape[0]):
        total = total + in_ref[i].astype(F32)
    out_ref[...] = total.astype(out_ref.dtype)


def renorm_body(half_ref, other_ref, start_ref, out_ref):
    start = start_ref[...].astype(F32)
    stepped = start + (half_ref[...] + other_ref[...])
    ratio = jnp.sqrt(jnp.mean(start * start, axis=-1, keepdims=True)) * lax.rsqrt(
        jnp.mean(stepped * stepped, axis=-1, keepdims=True) + 1e-06
    )
    fresh = (stepped * ratio).astype(BF16)
    for i in range(out_ref.shape[0]):
        out_ref[i] = fresh


def copies_body(in_ref, out_ref):
    for i in range(out_ref.shape[0]):
        out_ref[i] = in_ref[...]


def answer_body(q_ref, w_ref, out_ref):
    width = q_ref.shape[1]
    query = q_ref[...]
    gate_w, up_w, down_w = (w_ref[:, :, m].reshape(width, width) for m in range(3))
    gate = dot(query, gate_w, COLS_COLS)
    up = dot(query, up_w, COLS_COLS)
    hidden = (gate * jax.nn.sigmoid(gate) * up).astype(BF16)
    out_ref[...] = dot(hidden, down_w, COLS_COLS).astype(BF16).reshape(out_ref.shape)


def attend_body(place_ref, q_ref, *refs):
    *kv_refs, swap_ref, out_ref = refs
    rows = q_ref.shape[0]
    links = len(kv_refs)
    span = 2 * links * rows
    group = Q_HEADS // KV_HEADS
    kv_width = KV_HEADS * HEAD_DIM
    device, other = place_ref[0], place_ref[1]
    key = lax.broadcasted_iota(jnp.int32, (1, span), 1)
    s_pos = key + device * rows
    for i in range(1, 2 * links):
        origin = device - 2 * i if i < links else other - 2 * (i - links)
        s_pos = jnp.where(key >= i * rows, key + (origin - i) * rows, s_pos)
    t_pos = device * rows + lax.broadcasted_iota(jnp.int32, (rows, 1), 0)
    gap = t_pos - s_pos
    keep = (gap >= 0) & (gap < WINDOW) & (s_pos >= 0)
    keep = jnp.concatenate([keep] * group, axis=0)
    scaling = 1.0 / math.sqrt(HEAD_DIM)
    for c in range(KV_HEADS):
        own = slice(c * HEAD_DIM, (c + 1) * HEAD_DIM)
        vals = slice(kv_width + c * HEAD_DIM, kv_width + (c + 1) * HEAD_DIM)
        keys = jnp.concatenate([r[:, own] for r in kv_refs] + [swap_ref[:, own]], axis=0)
        values = jnp.concatenate([r[:, vals] for r in kv_refs] + [swap_ref[:, vals]], axis=0)
        heads = [slice((c * group + j) * HEAD_DIM, (c * group + j + 1) * HEAD_DIM) for j in range(group)]
        query = jnp.concatenate([q_ref[:, h] for h in heads], axis=0)
        scores = jnp.where(keep, dot(query, keys, COLS_COLS) * scaling, -1e30)
        expo = jnp.exp(scores - jnp.max(scores, axis=-1, keepdims=True))
        probs = (expo / jnp.sum(expo, axis=-1, keepdims=True)).astype(BF16)
        result = dot(probs, values)
        for j, h in enumerate(heads):
            out_ref[:, h] = result[j * rows : (j + 1) * rows]


def mix_body(attn_ref, fw_ref, out_ref):
    width = fw_ref.shape[2]
    for h in range(fw_ref.shape[0]):
        cols = slice(h * width, (h + 1) * width)
        out_ref[:, cols] = (attn_ref[:, cols] + fw_ref[h].astype(F32)).astype(BF16)


def on_device(
    fw_query, fw_key, fw_value, learn_rate, fast_weights, attn_query, attn_key, attn_value
):
    rows = attn_query.shape[0]
    tok_rows, width = fw_key.shape
    weights = fast_weights[:, 0]
    close, far = lax.axis_size(NEAR), lax.axis_size(FAR)
    part = width // (close * far)
    shape = jax.ShapeDtypeStruct
    product = 2 * tok_rows * width * width

    kv = [jnp.concatenate([attn_key, attn_value], axis=1)]
    hbm = pl.BlockSpec(memory_space=pltpu.HBM)
    vmem = pl.BlockSpec(memory_space=pltpu.VMEM)
    pieces = pl.pallas_call(
        grads_body,
        out_shape=shape((close, far, 3, part, width), BF16),
        in_specs=[hbm, hbm, vmem, hbm],
        out_specs=hbm,
        scratch_shapes=[
            pltpu.VMEM((tok_rows, width), BF16),
            pltpu.VMEM((tok_rows, width), BF16),
            pltpu.VMEM((3, width, width), BF16),
            pltpu.VMEM((3, close, far, part, width), BF16),
            pltpu.SemaphoreType.DMA((5,)),
            pltpu.SemaphoreType.DMA((3,)),
        ],
        compiler_params=pltpu.CompilerParams(vmem_limit_bytes=60 * MIB),
        cost_estimate=pl.CostEstimate(flops=6 * product, bytes_accessed=4 * MIB, transcendentals=0),
    )(fw_key, fw_value, learn_rate.reshape(1, tok_rows), weights)
    pieces = lax.all_to_all(pieces, NEAR, 0, 0, tiled=True)
    kv.append(next_chip(kv[-1]))
    pieces, kv[-1] = after(pieces, kv[-1])
    pieces = call(sum_body, shape((far, 3, part, width), BF16), (pieces,), 16)
    pieces = lax.all_to_all(pieces, FAR, 0, 0, tiled=True)
    half = call(sum_body, shape((3, part, width), F32), (pieces,), 16)

    mine = (lax.axis_index(NEAR) * far + lax.axis_index(FAR)) * part
    start = lax.dynamic_slice_in_dim(weights, mine, part, 2).transpose(0, 2, 1)
    other = swapped(half, "yh")
    kv.append(next_chip(kv[-1]))
    other, kv[-1] = after(other, kv[-1])
    fresh = call(renorm_body, shape((far, 3, part, width), BF16), (half, other, start), 16)
    fresh = lax.all_to_all(fresh, FAR, 0, 0, tiled=True)
    kv.append(next_chip(kv[-1]))
    fresh, kv[-1] = after(fresh, kv[-1])
    fresh = call(copies_body, shape((close, far, 3, part, width), BF16), (fresh,), 16)
    fresh = lax.all_to_all(fresh, NEAR, 0, 0, tiled=True)
    swap = swapped(jnp.concatenate(kv), "core")

    fw_out = call(
        answer_body,
        shape((tok_rows // rows, rows, width), BF16),
        (fw_query, fresh),
        24,
        3 * product,
    )
    fw_fine = lax.all_to_all(fw_out, HEAD, 0, 0, tiled=True)
    device = lax.axis_index(SEQ + HEAD)
    place = jnp.stack([device, device + 1 - 2 * lax.axis_index("core")])
    attn = pl.pallas_call(
        attend_body,
        out_shape=shape(attn_query.shape, F32),
        in_specs=[pl.BlockSpec(memory_space=pltpu.SMEM)]
        + [pl.BlockSpec(memory_space=pltpu.VMEM)] * (len(kv) + 2),
        compiler_params=pltpu.CompilerParams(vmem_limit_bytes=24 * MIB),
        cost_estimate=pl.CostEstimate(flops=10**9, bytes_accessed=3 * MIB, transcendentals=0),
    )(place, attn_query, *kv, swap)
    return call(mix_body, shape(attn_query.shape, BF16), (attn, fw_fine), 16)


def solution(mesh):
    fine = Mesh(
        mesh.devices.reshape([size for _, size in FINE]), tuple(name for name, _ in FINE)
    )
    placed = (
        P(SEQ, HEAD),
        P(SEQ, HEAD),
        P(SEQ, HEAD),
        P(SEQ, HEAD),
        P(None, HEAD, None, None),
        P(SEQ + HEAD, None),
        P(SEQ + HEAD, None),
        P(SEQ + HEAD, None),
    )
    return jax.shard_map(
        on_device, mesh=fine, in_specs=placed, out_specs=P(SEQ + HEAD, None), check_vma=False
    )
```

```python
import functools
import math

import jax
import jax.numpy as jnp
from jax import lax
from jax.experimental import pallas as pl
from jax.experimental.pallas import tpu as pltpu
from jax.sharding import Mesh, PartitionSpec as P

Q_HEADS = 32
KV_HEADS = 8
HEAD_DIM = 128
WINDOW = 256
MIB = 1 << 20

FINE = (("yh", 2), ("zh", 4), ("zl", 2), ("x", 4), ("yl", 4), ("core", 2))
SEQ = ("yh", "zh", "zl", "x")
HEAD = ("yl", "core")
NEAR = ("zl", "x")
FAR = ("zh",)

F32 = jnp.float32
BF16 = jnp.bfloat16
ROWS_ROWS = (((0,), (0,)), ((), ()))
COLS_COLS = (((1,), (1,)), ((), ()))


def next_step(value):
    steps = lax.axis_size(SEQ)
    return lax.ppermute(value, SEQ, [(i, i + 1) for i in range(steps - 1)])


def across(own, before, away):
    chips = lax.axis_size("yl")
    place = lax.axis_index("yl")
    block = jnp.where((place ^ away) > place, own, before)
    return lax.ppermute(block, "yl", [(i, i ^ away) for i in range(chips)])


def swapped(value, axis):
    return lax.ppermute(value, axis, [(0, 1), (1, 0)])


def after(value, first):
    return lax.optimization_barrier((value, first))


def call(body, out, args, mib, flops=0):
    moved = sum(a.size * a.dtype.itemsize for a in args) + out.size * out.dtype.itemsize
    return pl.pallas_call(
        body,
        out_shape=out,
        compiler_params=pltpu.CompilerParams(vmem_limit_bytes=mib * MIB),
        cost_estimate=pl.CostEstimate(flops=flops, bytes_accessed=moved, transcendentals=0),
    )(*args)


def dot(left, right, dims=(((1,), (0,)), ((), ()))):
    return lax.dot_general(left, right, dims, preferred_element_type=F32)


def grads_body(
    k_hbm, v_hbm, rate_ref, w_hbm, out_hbm, k_ref, v_ref, w_ref, out_ref, in_sems, out_sems
):
    close, far, _, part, width = out_hbm.shape
    sources = (k_hbm, w_hbm.at[0], w_hbm.at[1], v_hbm, w_hbm.at[2])
    targets = (k_ref, w_ref.at[0], w_ref.at[1], v_ref, w_ref.at[2])
    copies = [
        pltpu.make_async_copy(source, target, in_sems.at[i])
        for i, (source, target) in enumerate(zip(sources, targets))
    ]
    for copy in copies:
        copy.start()

    def send(m, left, right):
        grad = dot(left, right, ROWS_ROWS).astype(BF16)
        out_ref[m] = grad.reshape(close, far, part, width)
        copy = pltpu.make_async_copy(out_ref.at[m], out_hbm.at[:, :, m], out_sems.at[m])
        copy.start()
        return copy

    copies[0].wait()
    copies[1].wait()
    keys = k_ref[...]
    gate = dot(keys, w_ref[0])
    copies[2].wait()
    up = dot(keys, w_ref[1])
    copies[3].wait()
    rates = rate_ref[...].reshape(keys.shape[0], 1)
    scaled = (rates * v_ref[...].astype(F32)).astype(BF16)
    sigm = jax.nn.sigmoid(gate)
    act = gate * sigm
    sent = [send(2, scaled, (act * up).astype(BF16))]
    copies[4].wait()
    back = dot(scaled, w_ref[2], COLS_COLS)
    sent.append(send(1, (back * act).astype(BF16), keys))
    d_gate = (back * up * sigm * (1.0 + gate * (1.0 - sigm))).astype(BF16)
    sent.append(send(0, d_gate, keys))
    for copy in sent:
        copy.wait()


def sum_body(in_ref, out_ref):
    total = in_ref[0].astype(F32)
    for i in range(1, in_ref.shape[0]):
        total = total + in_ref[i].astype(F32)
    out_ref[...] = total.astype(out_ref.dtype)


def renorm_body(half_ref, other_ref, start_ref, out_ref):
    start = start_ref[...].astype(F32)
    stepped = start + (half_ref[...] + other_ref[...])
    ratio = jnp.sqrt(jnp.mean(start * start, axis=-1, keepdims=True)) * lax.rsqrt(
        jnp.mean(stepped * stepped, axis=-1, keepdims=True) + 1e-06
    )
    fresh = (stepped * ratio).astype(BF16)
    for i in range(out_ref.shape[0]):
        out_ref[i] = fresh


def copies_body(in_ref, out_ref):
    for i in range(out_ref.shape[0]):
        out_ref[i] = in_ref[...]


def answer_body(q_ref, w_ref, out_ref):
    width = q_ref.shape[1]
    query = q_ref[...]
    gate_w, up_w, down_w = (w_ref[:, :, m].reshape(width, width) for m in range(3))
    gate = dot(query, gate_w, COLS_COLS)
    up = dot(query, up_w, COLS_COLS)
    hidden = (gate * jax.nn.sigmoid(gate) * up).astype(BF16)
    out_ref[...] = dot(hidden, down_w, COLS_COLS).astype(BF16).reshape(out_ref.shape)


def attend_body(place_ref, q_ref, *refs):
    *kv_refs, swap_ref, out_ref = refs
    rows = q_ref.shape[0]
    links = len(kv_refs)
    span = 2 * links * rows
    group = Q_HEADS // KV_HEADS
    kv_width = KV_HEADS * HEAD_DIM
    device = place_ref[0]
    key = lax.broadcasted_iota(jnp.int32, (1, span), 1)
    s_pos = key + place_ref[0] * rows
    for i in range(1, 2 * links):
        s_pos = jnp.where(key >= i * rows, key + (place_ref[i] - i) * rows, s_pos)
    t_pos = device * rows + lax.broadcasted_iota(jnp.int32, (rows, 1), 0)
    gap = t_pos - s_pos
    keep = (gap >= 0) & (gap < WINDOW) & (s_pos >= 0)
    keep = jnp.concatenate([keep] * group, axis=0)
    scaling = 1.0 / math.sqrt(HEAD_DIM)
    for c in range(KV_HEADS):
        own = slice(c * HEAD_DIM, (c + 1) * HEAD_DIM)
        vals = slice(kv_width + c * HEAD_DIM, kv_width + (c + 1) * HEAD_DIM)
        keys = jnp.concatenate([r[:, own] for r in kv_refs] + [swap_ref[:, own]], axis=0)
        values = jnp.concatenate([r[:, vals] for r in kv_refs] + [swap_ref[:, vals]], axis=0)
        heads = [slice((c * group + j) * HEAD_DIM, (c * group + j + 1) * HEAD_DIM) for j in range(group)]
        query = jnp.concatenate([q_ref[:, h] for h in heads], axis=0)
        scores = jnp.where(keep, dot(query, keys, COLS_COLS) * scaling, -1e30)
        expo = jnp.exp(scores - jnp.max(scores, axis=-1, keepdims=True))
        probs = (expo / jnp.sum(expo, axis=-1, keepdims=True)).astype(BF16)
        result = dot(probs, values)
        for j, h in enumerate(heads):
            out_ref[:, h] = result[j * rows : (j + 1) * rows]


def mix_body(attn_ref, fw_ref, out_ref):
    width = fw_ref.shape[2]
    for h in range(fw_ref.shape[0]):
        cols = slice(h * width, (h + 1) * width)
        out_ref[:, cols] = (attn_ref[:, cols] + fw_ref[h].astype(F32)).astype(BF16)


def on_device(
    fw_query, fw_key, fw_value, learn_rate, fast_weights, attn_query, attn_key, attn_value
):
    rows = attn_query.shape[0]
    tok_rows, width = fw_key.shape
    weights = fast_weights[:, 0]
    close, far = lax.axis_size(NEAR), lax.axis_size(FAR)
    part = width // (close * far)
    shape = jax.ShapeDtypeStruct
    product = 2 * tok_rows * width * width

    kv = [jnp.concatenate([attn_key, attn_value], axis=1)]
    hbm = pl.BlockSpec(memory_space=pltpu.HBM)
    vmem = pl.BlockSpec(memory_space=pltpu.VMEM)
    pieces = pl.pallas_call(
        grads_body,
        out_shape=shape((close, far, 3, part, width), BF16),
        in_specs=[hbm, hbm, vmem, hbm],
        out_specs=hbm,
        scratch_shapes=[
            pltpu.VMEM((tok_rows, width), BF16),
            pltpu.VMEM((tok_rows, width), BF16),
            pltpu.VMEM((3, width, width), BF16),
            pltpu.VMEM((3, close, far, part, width), BF16),
            pltpu.SemaphoreType.DMA((5,)),
            pltpu.SemaphoreType.DMA((3,)),
        ],
        compiler_params=pltpu.CompilerParams(vmem_limit_bytes=60 * MIB),
        cost_estimate=pl.CostEstimate(flops=6 * product, bytes_accessed=4 * MIB, transcendentals=0),
    )(fw_key, fw_value, learn_rate.reshape(1, tok_rows), weights)
    pieces = lax.all_to_all(pieces, NEAR, 0, 0, tiled=True)
    before = next_step(kv[0])
    pieces, before = after(pieces, before)
    pieces = call(sum_body, shape((far, 3, part, width), BF16), (pieces,), 16)
    pieces = lax.all_to_all(pieces, FAR, 0, 0, tiled=True)
    half = call(sum_body, shape((3, part, width), F32), (pieces,), 16)

    mine = (lax.axis_index(NEAR) * far + lax.axis_index(FAR)) * part
    start = lax.dynamic_slice_in_dim(weights, mine, part, 2).transpose(0, 2, 1)
    other = swapped(half, "yh")
    kv += [across(kv[0], before, 1)]
    other, kv[-1:] = after(other, kv[-1:])
    fresh = call(renorm_body, shape((far, 3, part, width), BF16), (half, other, start), 16)
    fresh = lax.all_to_all(fresh, FAR, 0, 0, tiled=True)
    kv += [across(kv[0], before, 2)]
    fresh, kv[-1:] = after(fresh, kv[-1:])
    fresh = call(copies_body, shape((close, far, 3, part, width), BF16), (fresh,), 16)
    fresh = lax.all_to_all(fresh, NEAR, 0, 0, tiled=True)
    kv += [across(kv[0], before, 3)]
    swap = swapped(jnp.concatenate(kv), "core")

    fw_out = call(
        answer_body,
        shape((tok_rows // rows, rows, width), BF16),
        (fw_query, fresh),
        24,
        3 * product,
    )
    fw_fine = lax.all_to_all(fw_out, HEAD, 0, 0, tiled=True)
    chip, core = lax.axis_index("yl"), lax.axis_index("core")
    heads = lax.axis_size(HEAD)
    place = jnp.stack(
        [
            (lax.axis_index(SEQ) - ((chip ^ away) > chip).astype(jnp.int32)) * heads
            + 2 * (chip ^ away)
            + side
            for side in (core, 1 - core)
            for away in range(4)
        ]
    )
    attn = pl.pallas_call(
        attend_body,
        out_shape=shape(attn_query.shape, F32),
        in_specs=[pl.BlockSpec(memory_space=pltpu.SMEM)]
        + [pl.BlockSpec(memory_space=pltpu.VMEM)] * (len(kv) + 2),
        compiler_params=pltpu.CompilerParams(vmem_limit_bytes=24 * MIB),
        cost_estimate=pl.CostEstimate(flops=10**9, bytes_accessed=3 * MIB, transcendentals=0),
    )(place, attn_query, *kv, swap)
    return call(mix_body, shape(attn_query.shape, BF16), (attn, fw_fine), 16)


def solution(mesh):
    fine = Mesh(
        mesh.devices.reshape([size for _, size in FINE]), tuple(name for name, _ in FINE)
    )
    placed = (
        P(SEQ, HEAD),
        P(SEQ, HEAD),
        P(SEQ, HEAD),
        P(SEQ, HEAD),
        P(None, HEAD, None, None),
        P(SEQ + HEAD, None),
        P(SEQ + HEAD, None),
        P(SEQ + HEAD, None),
    )
    return jax.shard_map(
        on_device, mesh=fine, in_specs=placed, out_specs=P(SEQ + HEAD, None), check_vma=False
    )
```

```python
import functools
import math

import jax
import jax.numpy as jnp
from jax import lax
from jax.experimental import pallas as pl
from jax.experimental.pallas import tpu as pltpu
from jax.sharding import Mesh, PartitionSpec as P

Q_HEADS = 32
KV_HEADS = 8
HEAD_DIM = 128
WINDOW = 256
MIB = 1 << 20

FINE = (("yh", 2), ("zh", 4), ("zl", 2), ("x", 4), ("yl", 4), ("core", 2))
SEQ = ("yh", "zh", "zl", "x")
HEAD = ("yl", "core")
NEAR = ("zl", "x")
FAR = ("zh",)

F32 = jnp.float32
BF16 = jnp.bfloat16
ROWS_ROWS = (((0,), (0,)), ((), ()))
COLS_COLS = (((1,), (1,)), ((), ()))


def next_step(value):
    steps = lax.axis_size(SEQ)
    return lax.ppermute(value, SEQ, [(i, i + 1) for i in range(steps - 1)])


def across(own, before, away):
    chips = lax.axis_size("yl")
    place = lax.axis_index("yl")
    block = jnp.where((place ^ away) > place, own, before)
    return lax.ppermute(block, "yl", [(i, i ^ away) for i in range(chips)])


def swapped(value, axis):
    return lax.ppermute(value, axis, [(0, 1), (1, 0)])


def after(value, first):
    return lax.optimization_barrier((value, first))


def call(body, out, args, mib, flops=0):
    moved = sum(a.size * a.dtype.itemsize for a in args) + out.size * out.dtype.itemsize
    return pl.pallas_call(
        body,
        out_shape=out,
        compiler_params=pltpu.CompilerParams(vmem_limit_bytes=mib * MIB),
        cost_estimate=pl.CostEstimate(flops=flops, bytes_accessed=moved, transcendentals=0),
    )(*args)


def dot(left, right, dims=(((1,), (0,)), ((), ()))):
    return lax.dot_general(left, right, dims, preferred_element_type=F32)


def grads_body(
    k_hbm, v_hbm, rate_ref, w_hbm, out_hbm, k_ref, v_ref, w_ref, out_ref, in_sems, out_sems
):
    close, far, _, part, width = out_hbm.shape
    sources = (k_hbm, w_hbm.at[0], w_hbm.at[1], v_hbm, w_hbm.at[2])
    targets = (k_ref, w_ref.at[0], w_ref.at[1], v_ref, w_ref.at[2])
    copies = [
        pltpu.make_async_copy(source, target, in_sems.at[i])
        for i, (source, target) in enumerate(zip(sources, targets))
    ]
    for copy in copies:
        copy.start()

    def send(m, left, right):
        grad = dot(left, right, ROWS_ROWS).astype(BF16)
        out_ref[m] = grad.reshape(close, far, part, width)
        copy = pltpu.make_async_copy(out_ref.at[m], out_hbm.at[:, :, m], out_sems.at[m])
        copy.start()
        return copy

    copies[0].wait()
    copies[1].wait()
    keys = k_ref[...]
    gate = dot(keys, w_ref[0])
    copies[2].wait()
    up = dot(keys, w_ref[1])
    copies[3].wait()
    rates = rate_ref[...].reshape(keys.shape[0], 1)
    scaled = (rates * v_ref[...].astype(F32)).astype(BF16)
    sigm = jax.nn.sigmoid(gate)
    act = gate * sigm
    sent = [send(2, scaled, (act * up).astype(BF16))]
    copies[4].wait()
    back = dot(scaled, w_ref[2], COLS_COLS)
    sent.append(send(1, (back * act).astype(BF16), keys))
    d_gate = (back * up * sigm * (1.0 + gate * (1.0 - sigm))).astype(BF16)
    sent.append(send(0, d_gate, keys))
    for copy in sent:
        copy.wait()


def sum_body(in_ref, out_ref):
    total = in_ref[0].astype(F32)
    for i in range(1, in_ref.shape[0]):
        total = total + in_ref[i].astype(F32)
    out_ref[...] = total.astype(out_ref.dtype)


def renorm_body(half_ref, other_ref, start_ref, out_ref):
    start = start_ref[...].astype(F32)
    stepped = start + (half_ref[...] + other_ref[...])
    ratio = jnp.sqrt(jnp.mean(start * start, axis=-1, keepdims=True)) * lax.rsqrt(
        jnp.mean(stepped * stepped, axis=-1, keepdims=True) + 1e-06
    )
    fresh = (stepped * ratio).astype(BF16)
    for i in range(out_ref.shape[0]):
        out_ref[i] = fresh


def copies_body(in_ref, out_ref):
    for i in range(out_ref.shape[0]):
        out_ref[i] = in_ref[...]


def answer_body(q_ref, w_ref, out_ref):
    width = q_ref.shape[1]
    query = q_ref[...]
    gate_w, up_w, down_w = (w_ref[:, :, m].reshape(width, width) for m in range(3))
    gate = dot(query, gate_w, COLS_COLS)
    up = dot(query, up_w, COLS_COLS)
    hidden = (gate * jax.nn.sigmoid(gate) * up).astype(BF16)
    out_ref[...] = dot(hidden, down_w, COLS_COLS).astype(BF16).reshape(out_ref.shape)


def attend_body(place_ref, q_ref, *refs):
    *kv_refs, swap_ref, out_ref = refs
    rows = q_ref.shape[0]
    links = len(kv_refs)
    span = 2 * links * rows
    group = Q_HEADS // KV_HEADS
    kv_width = KV_HEADS * HEAD_DIM
    device = place_ref[0]
    key = lax.broadcasted_iota(jnp.int32, (1, span), 1)
    s_pos = key + place_ref[0] * rows
    for i in range(1, 2 * links):
        s_pos = jnp.where(key >= i * rows, key + (place_ref[i] - i) * rows, s_pos)
    t_pos = device * rows + lax.broadcasted_iota(jnp.int32, (rows, 1), 0)
    gap = t_pos - s_pos
    keep = (gap >= 0) & (gap < WINDOW) & (s_pos >= 0)
    keep = jnp.concatenate([keep] * group, axis=0)
    scaling = 1.0 / math.sqrt(HEAD_DIM)
    for c in range(KV_HEADS):
        own = slice(c * HEAD_DIM, (c + 1) * HEAD_DIM)
        vals = slice(kv_width + c * HEAD_DIM, kv_width + (c + 1) * HEAD_DIM)
        keys = jnp.concatenate([r[:, own] for r in kv_refs] + [swap_ref[:, own]], axis=0)
        values = jnp.concatenate([r[:, vals] for r in kv_refs] + [swap_ref[:, vals]], axis=0)
        heads = [slice((c * group + j) * HEAD_DIM, (c * group + j + 1) * HEAD_DIM) for j in range(group)]
        query = jnp.concatenate([q_ref[:, h] for h in heads], axis=0)
        scores = jnp.where(keep, dot(query, keys, COLS_COLS) * scaling, -1e30)
        expo = jnp.exp(scores - jnp.max(scores, axis=-1, keepdims=True))
        probs = (expo / jnp.sum(expo, axis=-1, keepdims=True)).astype(BF16)
        result = dot(probs, values)
        for j, h in enumerate(heads):
            out_ref[:, h] = result[j * rows : (j + 1) * rows]


def mix_body(attn_ref, fw_ref, out_ref):
    width = fw_ref.shape[2]
    for h in range(fw_ref.shape[0]):
        cols = slice(h * width, (h + 1) * width)
        out_ref[:, cols] = (attn_ref[:, cols] + fw_ref[h].astype(F32)).astype(BF16)


def on_device(
    fw_query, fw_key, fw_value, learn_rate, fast_weights, attn_query, attn_key, attn_value
):
    rows = attn_query.shape[0]
    tok_rows, width = fw_key.shape
    weights = fast_weights[:, 0]
    close, far = lax.axis_size(NEAR), lax.axis_size(FAR)
    part = width // (close * far)
    shape = jax.ShapeDtypeStruct
    product = 2 * tok_rows * width * width

    kv = [jnp.concatenate([attn_key, attn_value], axis=1)]
    hbm = pl.BlockSpec(memory_space=pltpu.HBM)
    vmem = pl.BlockSpec(memory_space=pltpu.VMEM)
    pieces = pl.pallas_call(
        grads_body,
        out_shape=shape((close, far, 3, part, width), BF16),
        in_specs=[hbm, hbm, vmem, hbm],
        out_specs=hbm,
        scratch_shapes=[
            pltpu.VMEM((tok_rows, width), BF16),
            pltpu.VMEM((tok_rows, width), BF16),
            pltpu.VMEM((3, width, width), BF16),
            pltpu.VMEM((3, close, far, part, width), BF16),
            pltpu.SemaphoreType.DMA((5,)),
            pltpu.SemaphoreType.DMA((3,)),
        ],
        compiler_params=pltpu.CompilerParams(vmem_limit_bytes=60 * MIB),
        cost_estimate=pl.CostEstimate(flops=6 * product, bytes_accessed=4 * MIB, transcendentals=0),
    )(fw_key, fw_value, learn_rate.reshape(1, tok_rows), weights)
    pieces = lax.all_to_all(pieces, NEAR, 0, 0, tiled=True)
    before = next_step(kv[0])
    pieces = call(sum_body, shape((far, 3, part, width), BF16), (pieces,), 16)
    pieces = lax.all_to_all(pieces, FAR, 0, 0, tiled=True)
    half = call(sum_body, shape((3, part, width), F32), (pieces,), 16)

    mine = (lax.axis_index(NEAR) * far + lax.axis_index(FAR)) * part
    start = lax.dynamic_slice_in_dim(weights, mine, part, 2).transpose(0, 2, 1)
    other = swapped(half, "yh")
    kv += [across(kv[0], before, 1)]
    fresh = call(renorm_body, shape((far, 3, part, width), BF16), (half, other, start), 16)
    fresh, kv[-1:] = after(fresh, kv[-1:])
    fresh = lax.all_to_all(fresh, FAR, 0, 0, tiled=True)
    kv += [across(kv[0], before, 2)]
    fresh, kv[-1:] = after(fresh, kv[-1:])
    fresh = call(copies_body, shape((close, far, 3, part, width), BF16), (fresh,), 16)
    fresh = lax.all_to_all(fresh, NEAR, 0, 0, tiled=True)
    early = swapped(jnp.concatenate(kv[:3]), "core")
    kv += [across(kv[0], before, 3)]
    fresh, kv, early = (lambda t: (t[0], t[1][0], t[1][1]))(after(fresh, (kv, early)))

    fw_out = call(
        answer_body,
        shape((tok_rows // rows, rows, width), BF16),
        (fw_query, fresh),
        24,
        3 * product,
    )
    fw_out, kv = after(fw_out, kv)
    swap = jnp.concatenate([early, swapped(kv[3], "core")])
    fw_fine = lax.all_to_all(fw_out, HEAD, 0, 0, tiled=True)
    chip, core = lax.axis_index("yl"), lax.axis_index("core")
    heads = lax.axis_size(HEAD)
    place = jnp.stack(
        [
            (lax.axis_index(SEQ) - ((chip ^ away) > chip).astype(jnp.int32)) * heads
            + 2 * (chip ^ away)
            + side
            for side in (core, 1 - core)
            for away in range(4)
        ]
    )
    attn = pl.pallas_call(
        attend_body,
        out_shape=shape(attn_query.shape, F32),
        in_specs=[pl.BlockSpec(memory_space=pltpu.SMEM)]
        + [pl.BlockSpec(memory_space=pltpu.VMEM)] * (len(kv) + 2),
        compiler_params=pltpu.CompilerParams(vmem_limit_bytes=24 * MIB),
        cost_estimate=pl.CostEstimate(flops=10**9, bytes_accessed=3 * MIB, transcendentals=0),
    )(place, attn_query, *kv, swap)
    return call(mix_body, shape(attn_query.shape, BF16), (attn, fw_fine), 16)


def solution(mesh):
    fine = Mesh(
        mesh.devices.reshape([size for _, size in FINE]), tuple(name for name, _ in FINE)
    )
    placed = (
        P(SEQ, HEAD),
        P(SEQ, HEAD),
        P(SEQ, HEAD),
        P(SEQ, HEAD),
        P(None, HEAD, None, None),
        P(SEQ + HEAD, None),
        P(SEQ + HEAD, None),
        P(SEQ + HEAD, None),
    )
    return jax.shard_map(
        on_device, mesh=fine, in_specs=placed, out_specs=P(SEQ + HEAD, None), check_vma=False
    )
```
